32 devices in a mesh: blk: 8 (over z, x), grp: 4 (over y, core).
Axes of the slice: x: 2, y: 2, z: 4, core: 2. Of those that a mesh axis runs over, the one named last changes fastest.
Arguments:
- factors: bfloat16 [2, 3072, 3072], P(None, 'blk', 'grp'), may hold values from -0.109375 to 0.109375
- lower_inverse: float32 [2, 3072, 128], P(None, 'blk'), may hold values from -1 to 2
- upper_inverse: float32 [2, 3072, 128], P(None, 'blk'), may hold values from -1 to 2
- right_side: float32 [2, 3072, 512], P(None, 'blk', 'grp'), may hold values from -6 to 6
Outputs:
- solution: float32 [2, 3072, 512], P(None, 'blk', 'grp')
The draws below stay inside these ranges and needn't reach their ends.
All inputs are finite; a program needn't handle non-finite values.
Results may differ from the reference program's by a relative error of at most 0.0027.
Values may be sent and summed in bfloat16 or wider, within the bound.
A program may use at most 128 MiB of HBM per device.

```python
import math
import jax
import jax.numpy as jnp
from jax import lax

B = 128
ROWS_LAYER = 3072
NRHS = 512


def inverse_table(key):
    shape = (2, ROWS_LAYER, B)
    rows = lax.broadcasted_iota(jnp.int32, shape, 1) % B
    cols = lax.broadcasted_iota(jnp.int32, shape, 2)
    ident = (rows == cols).astype(jnp.float32)
    noise = 0.35 * jax.random.normal(key, shape, jnp.float32)
    return ident + noise / math.sqrt(B)


def draw_lower_inverse(key, part):
    return inverse_table(jax.random.fold_in(key, 11))


def draw_upper_inverse(key, part):
    return inverse_table(jax.random.fold_in(key, 23))


def block_levels(own_key, dims, pieces, smallest, high):
    gain, own = 1.0, jax.random.fold_in(own_key, 6)
    for position, blocks in pieces:
        draws = jnp.exp(jax.random.uniform(jax.random.fold_in(own, position), (blocks,), jnp.float32, smallest / len(pieces), high / len(pieces)))
        gain = gain * jnp.repeat(draws, dims[position] // blocks).reshape([-1 if axis == position else 1 for axis in range(len(dims))])
    return gain


def centred(stream_key, extent, spread, most, split=(), dtype=jnp.bfloat16):
    drawn = spread * jax.random.normal(stream_key, extent, jnp.float32)
    if split:
        drawn = drawn * block_levels(stream_key, extent, split, -0.22, 0.18)
    return jnp.clip(drawn, -most, most).astype(dtype)


def setup_inputs(seed: int = 0) -> dict:
    streams_of = jax.random.split(jax.random.key(seed), 5)
    return {
        "factors": centred(streams_of[0], (2, ROWS_LAYER, ROWS_LAYER), ROWS_LAYER ** -0.5, 0.109375, ((1, 8), (2, 4))),
        "lower_inverse": draw_lower_inverse(jax.random.fold_in(streams_of[4], 71), 0),
        "upper_inverse": draw_upper_inverse(jax.random.fold_in(streams_of[4], 71), 0),
        "right_side": centred(streams_of[3], (2, ROWS_LAYER, NRHS), 1.0, 6.0, ((1, 8), (2, 4)), jnp.float32),
    }


def solve_blocks(inverse, resid):
    width = inverse.shape[1]
    count = inverse.shape[0] // width
    blocks = inverse.reshape(count, width, width)
    parts = resid.reshape(count, width, resid.shape[1])
    value = jnp.einsum("nab,nbc->nac", blocks, parts, precision=lax.Precision.HIGHEST, preferred_element_type=jnp.float32)
    return value.reshape(resid.shape)


def reference(factors, lower_inverse, upper_inverse, right_side):
    forward_first = solve_blocks(lower_inverse[0], right_side[0])
    low = forward_first.astype(jnp.bfloat16)
    coupling = jnp.dot(factors[0], low, preferred_element_type=jnp.float32)
    forward_second = solve_blocks(lower_inverse[1], right_side[1] - coupling)
    second = solve_blocks(upper_inverse[1], forward_second)
    high = second.astype(jnp.bfloat16)
    coupling = jnp.dot(factors[1], high, preferred_element_type=jnp.float32)
    first = solve_blocks(upper_inverse[0], forward_first - coupling)
    return jnp.stack([first, second])
```

```python
import functools

import jax
import jax.numpy as jnp
from jax import lax
from jax.experimental import pallas as pl
from jax.experimental.pallas import tpu as pltpu
from jax.sharding import PartitionSpec as P

MESH = pl.DeviceIdType.MESH
CHUNKS = 2


def solve(inverse, resid, width):
    parts = [
        jnp.dot(
            inverse[n * width : (n + 1) * width],
            resid[n * width : (n + 1) * width],
            precision=lax.Precision.HIGHEST,
            preferred_element_type=jnp.float32,
        )
        for n in range(inverse.shape[0] // width)
    ]
    return jnp.concatenate(parts, axis=0)


def compose(left, right, width):
    return solve(left, right, width)


def kernel(nb, f, dinv, einv, rhs, out, fg, low, high, fwd, both, g_send, g_recv, f_send, f_recv):
    b, g = lax.axis_index("blk"), lax.axis_index("grp")
    width = dinv.shape[2]
    rows, depth = f.shape[1], f.shape[2]
    per = depth // rows
    line = nb // 2
    piece = rows // CHUNKS

    barrier = pltpu.get_barrier_semaphore()
    for d in range(1, line):
        pl.semaphore_signal(barrier, inc=1, device_id={"blk": b ^ (2 * d)}, device_id_type=MESH)
    pl.semaphore_signal(barrier, inc=1, device_id={"blk": b ^ 1}, device_id_type=MESH)
    for s in (1, 2):
        pl.semaphore_signal(barrier, inc=1, device_id={"grp": g ^ s}, device_id_type=MESH)

    first = solve(dinv[0], rhs[0], width)
    fwd[...] = first
    low[b] = first.astype(jnp.bfloat16)
    pl.semaphore_wait(barrier, line + 2)

    def block_copy(buf, layer, source, slot, peer):
        return pltpu.make_async_remote_copy(
            src_ref=buf.at[source],
            dst_ref=buf.at[source],
            send_sem=g_send.at[layer, slot],
            recv_sem=g_recv.at[layer, source],
            device_id={"blk": peer},
            device_id_type=MESH,
        )

    def gather_start(buf, layer):
        block_copy(buf, layer, b, 0, b ^ 1).start()
        for d in range(1, line):
            block_copy(buf, layer, b, d, b ^ (2 * d)).start()

    def gather_forward(buf, layer):
        for d in range(1, line):
            source = b ^ (2 * d)
            block_copy(buf, layer, source, 0, b ^ 1).wait_recv()
            block_copy(buf, layer, source, line - 1 + d, b ^ 1).start()

    def gather_wait(buf, layer):
        for d in range(line):
            block_copy(buf, layer, b ^ (2 * d) ^ 1, 0, b ^ 1).wait_recv()

    def gather_drain(buf, layer):
        for slot in range(2 * line - 1):
            block_copy(buf, layer, b, slot, b ^ 1).wait_send()

    def near(layer):
        return pltpu.make_async_remote_copy(
            src_ref=f.at[layer],
            dst_ref=fg.at[layer, 0],
            send_sem=f_send.at[layer, 2 * CHUNKS],
            recv_sem=f_recv.at[layer, 2 * CHUNKS],
            device_id={"grp": g ^ 1},
            device_id_type=MESH,
        )

    def across(layer, i):
        return pltpu.make_async_remote_copy(
            src_ref=f.at[layer, pl.ds(i * piece, piece)],
            dst_ref=fg.at[layer, 1, pl.ds(i * piece, piece)],
            send_sem=f_send.at[layer, i],
            recv_sem=f_recv.at[layer, i],
            device_id={"grp": g ^ 2},
            device_id_type=MESH,
        )

    def onward(layer, i):
        return pltpu.make_async_remote_copy(
            src_ref=fg.at[layer, 1, pl.ds(i * piece, piece)],
            dst_ref=fg.at[layer, 2, pl.ds(i * piece, piece)],
            send_sem=f_send.at[layer, CHUNKS + i],
            recv_sem=f_recv.at[layer, CHUNKS + i],
            device_id={"grp": g ^ 1},
            device_id_type=MESH,
        )

    def factor_forward(layer):
        for i in range(CHUNKS):
            across(layer, i).wait_recv()
            onward(layer, i).start()

    def factor_wait(layer):
        near(layer).wait_recv()
        for i in range(CHUNKS):
            onward(layer, i).wait_recv()

    def factor_drain(layer):
        near(layer).wait_send()
        for i in range(CHUNKS):
            onward(layer, i).wait_send()

    def couple(buf, layer):
        total = jnp.zeros((rows, buf.shape[2]), jnp.float32)
        for s in range(4):
            part = f.at[layer] if s == 0 else fg.at[layer, s - 1]
            start = (g ^ s) * per

            def step(j, total):
                at = pl.multiple_of(j * rows, rows)
                return total + jnp.dot(part[:, pl.ds(at, rows)], buf[start + j], preferred_element_type=jnp.float32)

            if per <= 4:
                for j in range(per):
                    total = step(j, total)
            else:
                total = lax.fori_loop(0, per, step, total)
        return total

    gather_start(low, 0)
    near(0).start()
    for i in range(CHUNKS):
        across(0, i).start()
    near(1).start()
    both[...] = compose(einv[1], dinv[1], width)
    gather_forward(low, 0)
    factor_forward(0)
    for i in range(CHUNKS):
        across(0, i).wait_send()
    for i in range(CHUNKS):
        across(1, i).start()
    gather_wait(low, 0)
    factor_wait(0)
    second = solve(both[...], rhs[1] - couple(low, 0), width)
    high[b] = second.astype(jnp.bfloat16)
    gather_start(high, 1)
    out[1] = second
    gather_drain(low, 0)
    factor_drain(0)
    gather_forward(high, 1)
    factor_forward(1)
    gather_wait(high, 1)
    factor_wait(1)
    out[0] = solve(einv[0], fwd[...] - couple(high, 1), width)
    gather_drain(high, 1)
    factor_drain(1)
    for i in range(CHUNKS):
        across(1, i).wait_send()


def solution(mesh):
    nb, ng = mesh.shape["blk"], mesh.shape["grp"]
    assert ng == 4 and nb & (nb - 1) == 0

    def local(factors, lower_inverse, upper_inverse, right_side):
        layers, rows, depth = factors.shape
        columns = right_side.shape[2]
        whole = pl.BlockSpec(memory_space=pltpu.VMEM)
        held = factors.size * 2 * 4 + nb * rows * columns * 4
        return pl.pallas_call(
            functools.partial(kernel, nb),
            out_shape=jax.ShapeDtypeStruct(right_side.shape, jnp.float32),
            in_specs=[whole] * 4,
            out_specs=whole,
            scratch_shapes=[
                pltpu.VMEM((layers, 3, rows, depth), jnp.bfloat16),
                pltpu.VMEM((nb, rows, columns), jnp.bfloat16),
                pltpu.VMEM((nb, rows, columns), jnp.bfloat16),
                pltpu.VMEM((rows, columns), jnp.float32),
                pltpu.VMEM(lower_inverse.shape[1:], jnp.float32),
                pltpu.SemaphoreType.DMA((layers, nb)),
                pltpu.SemaphoreType.DMA((layers, nb)),
                pltpu.SemaphoreType.DMA((layers, 2 * CHUNKS + 1)),
                pltpu.SemaphoreType.DMA((layers, 2 * CHUNKS + 1)),
            ],
            compiler_params=pltpu.CompilerParams(
                collective_id=0, has_side_effects=True, vmem_limit_bytes=held + 8 * 2**20
            ),
        )(factors, lower_inverse, upper_inverse, right_side)

    in_specs = (
        P(None, "blk", "grp"),
        P(None, "blk", None),
        P(None, "blk", None),
        P(None, "blk", "grp"),
    )
    return jax.shard_map(local, mesh=mesh, in_specs=in_specs, out_specs=P(None, "blk", "grp"), check_vma=False)
```

```python
import functools

import jax
import jax.numpy as jnp
from jax import lax
from jax.experimental import pallas as pl
from jax.experimental.pallas import tpu as pltpu
from jax.sharding import PartitionSpec as P

MESH = pl.DeviceIdType.MESH


def solve(inverse, resid, width):
    parts = [
        jnp.dot(
            inverse[n * width : (n + 1) * width],
            resid[n * width : (n + 1) * width],
            precision=lax.Precision.HIGHEST,
            preferred_element_type=jnp.float32,
        )
        for n in range(inverse.shape[0] // width)
    ]
    return jnp.concatenate(parts, axis=0)


def kernel(
    nb, f_hbm, dinv_hbm, einv_hbm, rhs_hbm, out,
    dinv, einv, rhs, fg, low, high, fwd, both, l_sem, g_send, g_recv, f_send, f_recv,
):
    b, g = lax.axis_index("blk"), lax.axis_index("grp")
    width = dinv.shape[2]
    rows, depth = fg.shape[2], fg.shape[3]
    per = depth // rows
    line = nb // 2
    at, side = b // 2, b % 2
    pieces, piece = rows // width, width

    barrier = pltpu.get_barrier_semaphore()

    def greet(**device):
        pl.semaphore_signal(barrier, inc=1, device_id=device, device_id_type=MESH)

    greet(blk=b ^ 1)
    greet(grp=g ^ 1)
    greet(grp=g ^ 2)

    greet(blk=(b + 2) % nb)
    greet(blk=(b + nb - 2) % nb)

    def load(i):
        source, target = (
            (dinv_hbm, dinv),
            (rhs_hbm, rhs),
            (einv_hbm, einv),
            (f_hbm.at[0], fg.at[0, 0]),
            (f_hbm.at[1], fg.at[1, 0]),
        )[i]
        return pltpu.make_async_copy(source, target, l_sem.at[i])

    for i in range(5):
        load(i).start()
    load(0).wait()
    load(1).wait()
    first = solve(dinv[0], rhs[0], width)
    fwd[...] = first
    low[b] = first.astype(jnp.bfloat16)
    pl.semaphore_wait(barrier, 5)

    def block_copy(buf, layer, source, way, half):
        peer = (b + 2, b - 2, b ^ 1)[way]
        window = pl.ds(half * piece, piece)
        return pltpu.make_async_remote_copy(
            src_ref=buf.at[source, window],
            dst_ref=buf.at[source, window],
            send_sem=g_send.at[layer, source, way, half],
            recv_sem=g_recv.at[layer, source, half],
            device_id={"blk": peer},
            device_id_type=MESH,
        )

    def onwards(buf, layer, source, half, ways, act):
        for way in ways:
            if way == 2:
                act(block_copy(buf, layer, source, way, half))
            else:
                @pl.when(at < line - 1 if way == 0 else at > 0)
                def _():
                    act(block_copy(buf, layer, source, way, half))

    def start(copy):
        copy.start()

    def gather_start(buf, layer, half):
        onwards(buf, layer, b, half, (0, 1, 2), start)

    def gather_forward(buf, layer, k, half):
        for way, there in ((0, at >= k), (1, at + k < line)):
            @pl.when(there)
            def _():
                source = b - 2 * k if way == 0 else b + 2 * k
                block_copy(buf, layer, source, 2, half).wait_recv()
                onwards(buf, layer, source, half, (way, 2), start)

    def gather_pass(buf, layer):
        def hop(k):
            for half in range(pieces):
                gather_forward(buf, layer, k, half)

        each(1, line, hop)

    def gather_wait(buf, layer, source):
        for half in range(pieces):
            block_copy(buf, layer, source, 2, half).wait_recv()

    def gather_drain(buf, layer):
        for half in range(pieces):
            onwards(buf, layer, b, half, (0, 1, 2), lambda copy: copy.wait_send())

            def step(k):
                for way, there in ((0, at >= k), (1, at + k < line)):
                    @pl.when(there)
                    def _():
                        source = b - 2 * k if way == 0 else b + 2 * k
                        onwards(buf, layer, source, half, (way, 2), lambda copy: copy.wait_send())

            each(1, line, step)

    def each(low_end, high_end, step):
        if high_end - low_end <= 8:
            for k in range(low_end, high_end):
                step(k)
        else:
            pl.loop(low_end, high_end)(step)

    def factor_copy(layer, source, target, slot, peer, i=None):
        if i is not None:
            source = source.at[pl.ds(i * piece, piece)]
            target = target.at[pl.ds(i * piece, piece)]
        return pltpu.make_async_remote_copy(
            src_ref=source,
            dst_ref=target,
            send_sem=f_send.at[layer, slot],
            recv_sem=f_recv.at[layer, slot],
            device_id={"grp": peer},
            device_id_type=MESH,
        )

    def near(layer):
        return factor_copy(layer, f_hbm.at[layer], fg.at[layer, 1], 2 * pieces, g ^ 1)

    def across(layer, i):
        return factor_copy(layer, f_hbm.at[layer], fg.at[layer, 2], i, g ^ 2, i)

    def onward(layer, i):
        return factor_copy(layer, fg.at[layer, 2], fg.at[layer, 3], pieces + i, g ^ 1, i)

    def factor_forward(layer, i):
        across(layer, i).wait_recv()
        onward(layer, i).start()

    def factor_drain(layer):
        near(layer).wait_send()
        for i in range(pieces):
            onward(layer, i).wait_send()

    def term(buf, layer, source):
        slot = (source // per) ^ g
        place = pl.multiple_of((source % per) * rows, rows)
        return jnp.dot(fg[layer, slot, :, pl.ds(place, rows)], buf[source], preferred_element_type=jnp.float32)

    def couple(low_end, high_end):
        window = slice(low_end, high_end)
        total = jnp.zeros((high_end - low_end, fwd.shape[1]), jnp.float32)
        for slot in range(4):
            first = (g ^ slot) * per

            def step(j, total):
                place = pl.ds(pl.multiple_of(j * rows, rows), rows)
                return total + jnp.dot(fg[0, slot, window, place], low[first + j], preferred_element_type=jnp.float32)

            if per <= 4:
                for j in range(per):
                    total = step(j, total)
            else:
                total = lax.fori_loop(0, per, step, total)
        return total

    def advance(first, last):
        for i in range(first, last):
            onward(0, i).wait_recv()
        window = slice(first * piece, last * piece)
        second = solve(both[window], rhs[1, window] - couple(first * piece, last * piece), width)
        high[b, window] = second.astype(jnp.bfloat16)
        for i in range(first, last):
            gather_start(high, 1, i)
        out[1, window] = second

    for i in range(pieces):
        across(0, i).start()
    for i in range(pieces):
        gather_start(low, 0, i)
    near(0).start()
    load(2).wait()
    both[...] = solve(einv[1], dinv[1], width)
    gather_pass(low, 0)
    near(1).start()
    for i in range(pieces - 1):
        factor_forward(0, i)
    for i in range(pieces):
        across(1, i).start()
    each(0, nb // 2, lambda k: gather_wait(low, 0, 2 * k + 1 - side))
    load(3).wait()
    near(0).wait_recv()
    advance(0, pieces - 1)
    factor_forward(0, pieces - 1)
    advance(pieces - 1, pieces)
    gather_pass(high, 1)
    for i in range(pieces):
        factor_forward(1, i)
    near(1).wait_recv()
    for i in range(pieces):
        onward(1, i).wait_recv()
    load(4).wait()
    for i in range(pieces):
        across(0, i).wait_send()
    gather_drain(low, 0)
    factor_drain(0)
    total = jnp.zeros(fwd.shape, jnp.float32)

    def mine(k, total):
        return total + term(high, 1, 2 * k + side)

    def theirs(k, total):
        source = b ^ 1 ^ (2 * k)
        gather_wait(high, 1, source)
        return total + term(high, 1, source)

    if line <= 8:
        for k in range(line):
            total = mine(k, total)
        for k in range(line):
            total = theirs(k, total)
    else:
        total = lax.fori_loop(0, line, mine, total)
        total = lax.fori_loop(0, line, theirs, total)
    out[0] = solve(einv[0], fwd[...] - total, width)
    gather_drain(high, 1)
    factor_drain(1)
    for i in range(pieces):
        across(1, i).wait_send()


def solution(mesh):
    nb, ng = mesh.shape["blk"], mesh.shape["grp"]
    assert ng == 4 and nb & (nb - 1) == 0

    def local(factors, lower_inverse, upper_inverse, right_side):
        layers, rows, depth = factors.shape
        columns = right_side.shape[2]
        whole = pl.BlockSpec(memory_space=pltpu.VMEM)
        apart = pl.BlockSpec(memory_space=pltpu.HBM)
        pieces = rows // lower_inverse.shape[2]
        held = factors.size * 2 * 4 + nb * rows * columns * 4
        return pl.pallas_call(
            functools.partial(kernel, nb),
            out_shape=jax.ShapeDtypeStruct(right_side.shape, jnp.float32),
            in_specs=[apart] * 4,
            out_specs=whole,
            scratch_shapes=[
                pltpu.VMEM(lower_inverse.shape, jnp.float32),
                pltpu.VMEM(upper_inverse.shape, jnp.float32),
                pltpu.VMEM(right_side.shape, jnp.float32),
                pltpu.VMEM((layers, 4, rows, depth), jnp.bfloat16),
                pltpu.VMEM((nb, rows, columns), jnp.bfloat16),
                pltpu.VMEM((nb, rows, columns), jnp.bfloat16),
                pltpu.VMEM((rows, columns), jnp.float32),
                pltpu.VMEM(lower_inverse.shape[1:], jnp.float32),
                pltpu.SemaphoreType.DMA((5,)),
                pltpu.SemaphoreType.DMA((layers, nb, 3, pieces)),
                pltpu.SemaphoreType.DMA((layers, nb, pieces)),
                pltpu.SemaphoreType.DMA((layers, 2 * pieces + 1)),
                pltpu.SemaphoreType.DMA((layers, 2 * pieces + 1)),
            ],
            compiler_params=pltpu.CompilerParams(
                collective_id=0, has_side_effects=True, vmem_limit_bytes=held + 8 * 2**20
            ),
        )(factors, lower_inverse, upper_inverse, right_side)

    in_specs = (
        P(None, "blk", "grp"),
        P(None, "blk", None),
        P(None, "blk", None),
        P(None, "blk", "grp"),
    )
    return jax.shard_map(local, mesh=mesh, in_specs=in_specs, out_specs=P(None, "blk", "grp"), check_vma=False)
```

```python
import functools

import jax
import jax.numpy as jnp
from jax import lax
from jax.experimental import pallas as pl
from jax.experimental.pallas import tpu as pltpu
from jax.sharding import PartitionSpec as P

MESH = pl.DeviceIdType.MESH


def solve(inverse, resid, width):
    parts = [
        jnp.dot(
            inverse[n * width : (n + 1) * width],
            resid[n * width : (n + 1) * width],
            precision=lax.Precision.HIGHEST,
            preferred_element_type=jnp.float32,
        )
        for n in range(inverse.shape[0] // width)
    ]
    return jnp.concatenate(parts, axis=0)


def kernel(
    nb, f_hbm, dinv_hbm, einv_hbm, rhs_hbm, out,
    dinv, einv, rhs, fg, low, high, fwd, both, l_sem, g_send, g_recv, f_send, f_recv,
):
    b, g = lax.axis_index("blk"), lax.axis_index("grp")
    width = dinv.shape[2]
    rows, depth = fg.shape[2], fg.shape[3]
    per = depth // rows
    line = nb // 2
    at, side = b // 2, b % 2
    pieces, piece = rows // width, width

    barrier = pltpu.get_barrier_semaphore()

    def greet(**device):
        pl.semaphore_signal(barrier, inc=1, device_id=device, device_id_type=MESH)

    greet(blk=b ^ 1)
    greet(grp=g ^ 1)
    greet(grp=g ^ 2)

    @pl.when(at > 0)
    def _():
        greet(blk=b - 2)

    @pl.when(at < line - 1)
    def _():
        greet(blk=b + 2)

    def load(i):
        source, target = (
            (dinv_hbm, dinv),
            (rhs_hbm, rhs),
            (einv_hbm, einv),
            (f_hbm.at[0], fg.at[0, 0]),
            (f_hbm.at[1], fg.at[1, 0]),
        )[i]
        return pltpu.make_async_copy(source, target, l_sem.at[i])

    for i in range(5):
        load(i).start()
    load(0).wait()
    load(1).wait()
    first = solve(dinv[0], rhs[0], width)
    fwd[...] = first
    low[b] = first.astype(jnp.bfloat16)
    pl.semaphore_wait(barrier, 3 + jnp.int32(at > 0) + jnp.int32(at < line - 1))

    def block_copy(buf, layer, source, way, half):
        peer = (b + 2, b - 2, b ^ 1)[way]
        window = pl.ds(half * piece, piece)
        return pltpu.make_async_remote_copy(
            src_ref=buf.at[source, window],
            dst_ref=buf.at[source, window],
            send_sem=g_send.at[layer, source, way, half],
            recv_sem=g_recv.at[layer, source, half],
            device_id={"blk": peer},
            device_id_type=MESH,
        )

    def onwards(buf, layer, source, half, ways, act):
        for way in ways:
            if way == 2:
                act(block_copy(buf, layer, source, way, half))
            else:
                @pl.when(at < line - 1 if way == 0 else at > 0)
                def _():
                    act(block_copy(buf, layer, source, way, half))

    def start(copy):
        copy.start()

    def gather_start(buf, layer, half):
        onwards(buf, layer, b, half, (0, 1, 2), start)

    def gather_forward(buf, layer, k, half):
        for way, there in ((0, at >= k), (1, at + k < line)):
            @pl.when(there)
            def _():
                source = b - 2 * k if way == 0 else b + 2 * k
                block_copy(buf, layer, source, 2, half).wait_recv()
                onwards(buf, layer, source, half, (way, 2), start)

    def gather_pass(buf, layer):
        def hop(k):
            for half in range(pieces):
                gather_forward(buf, layer, k, half)

        each(1, line, hop)

    def gather_wait(buf, layer, source):
        for half in range(pieces):
            block_copy(buf, layer, source, 2, half).wait_recv()

    def gather_drain(buf, layer):
        for half in range(pieces):
            onwards(buf, layer, b, half, (0, 1, 2), lambda copy: copy.wait_send())

            def step(k):
                for way, there in ((0, at >= k), (1, at + k < line)):
                    @pl.when(there)
                    def _():
                        source = b - 2 * k if way == 0 else b + 2 * k
                        onwards(buf, layer, source, half, (way, 2), lambda copy: copy.wait_send())

            each(1, line, step)

    def each(low_end, high_end, step):
        if high_end - low_end <= 8:
            for k in range(low_end, high_end):
                step(k)
        else:
            pl.loop(low_end, high_end)(step)

    def factor_copy(layer, source, target, slot, peer, i=None):
        if i is not None:
            source = source.at[pl.ds(i * piece, piece)]
            target = target.at[pl.ds(i * piece, piece)]
        return pltpu.make_async_remote_copy(
            src_ref=source,
            dst_ref=target,
            send_sem=f_send.at[layer, slot],
            recv_sem=f_recv.at[layer, slot],
            device_id={"grp": peer},
            device_id_type=MESH,
        )

    def near(layer):
        return factor_copy(layer, f_hbm.at[layer], fg.at[layer, 1], 2 * pieces, g ^ 1)

    def across(layer, i):
        return factor_copy(layer, f_hbm.at[layer], fg.at[layer, 2], i, g ^ 2, i)

    def onward(layer, i):
        return factor_copy(layer, fg.at[layer, 2], fg.at[layer, 3], pieces + i, g ^ 1, i)

    def factor_forward(layer, i):
        across(layer, i).wait_recv()
        onward(layer, i).start()

    def factor_drain(layer):
        near(layer).wait_send()
        for i in range(pieces):
            onward(layer, i).wait_send()

    def term(buf, layer, source):
        slot = (source // per) ^ g
        place = pl.multiple_of((source % per) * rows, rows)
        return jnp.dot(fg[layer, slot, :, pl.ds(place, rows)], buf[source], preferred_element_type=jnp.float32)

    def couple(low_end, high_end):
        window = slice(low_end, high_end)
        total = jnp.zeros((high_end - low_end, fwd.shape[1]), jnp.float32)
        for slot in range(4):
            first = (g ^ slot) * per

            def step(j, total):
                place = pl.ds(pl.multiple_of(j * rows, rows), rows)
                return total + jnp.dot(fg[0, slot, window, place], low[first + j], preferred_element_type=jnp.float32)

            if per <= 4:
                for j in range(per):
                    total = step(j, total)
            else:
                total = lax.fori_loop(0, per, step, total)
        return total

    def advance(first, last):
        for i in range(first, last):
            onward(0, i).wait_recv()
        window = slice(first * piece, last * piece)
        second = solve(both[window], rhs[1, window] - couple(first * piece, last * piece), width)
        high[b, window] = second.astype(jnp.bfloat16)
        for i in range(first, last):
            gather_start(high, 1, i)
        out[1, window] = second

    for i in range(pieces):
        across(0, i).start()
    for i in range(pieces):
        gather_start(low, 0, i)
    near(0).start()
    load(2).wait()
    both[...] = solve(einv[1], dinv[1], width)
    gather_pass(low, 0)
    near(1).start()
    for i in range(pieces - 1):
        factor_forward(0, i)
    for i in range(pieces):
        across(1, i).start()
    each(0, nb // 2, lambda k: gather_wait(low, 0, 2 * k + 1 - side))
    load(3).wait()
    near(0).wait_recv()
    advance(0, pieces - 1)
    factor_forward(0, pieces - 1)
    advance(pieces - 1, pieces)
    gather_pass(high, 1)
    for i in range(pieces):
        factor_forward(1, i)
    near(1).wait_recv()
    for i in range(pieces):
        onward(1, i).wait_recv()
    load(4).wait()
    total = jnp.zeros(fwd.shape, jnp.float32)

    def mine(k, total):
        return total + term(high, 1, 2 * k + side)

    def theirs(k, total):
        source = b ^ 1 ^ (2 * k)
        gather_wait(high, 1, source)
        return total + term(high, 1, source)

    if line <= 8:
        for k in range(line):
            total = mine(k, total)
        for k in range(line):
            total = theirs(k, total)
    else:
        total = lax.fori_loop(0, line, mine, total)
        total = lax.fori_loop(0, line, theirs, total)
    out[0] = solve(einv[0], fwd[...] - total, width)
    for i in range(pieces):
        across(0, i).wait_send()
    gather_drain(low, 0)
    factor_drain(0)
    gather_drain(high, 1)
    factor_drain(1)
    for i in range(pieces):
        across(1, i).wait_send()


def solution(mesh):
    nb, ng = mesh.shape["blk"], mesh.shape["grp"]
    assert ng == 4 and nb & (nb - 1) == 0

    def local(factors, lower_inverse, upper_inverse, right_side):
        layers, rows, depth = factors.shape
        columns = right_side.shape[2]
        whole = pl.BlockSpec(memory_space=pltpu.VMEM)
        apart = pl.BlockSpec(memory_space=pltpu.HBM)
        pieces = rows // lower_inverse.shape[2]
        held = factors.size * 2 * 4 + nb * rows * columns * 4
        return pl.pallas_call(
            functools.partial(kernel, nb),
            out_shape=jax.ShapeDtypeStruct(right_side.shape, jnp.float32),
            in_specs=[apart] * 4,
            out_specs=whole,
            scratch_shapes=[
                pltpu.VMEM(lower_inverse.shape, jnp.float32),
                pltpu.VMEM(upper_inverse.shape, jnp.float32),
                pltpu.VMEM(right_side.shape, jnp.float32),
                pltpu.VMEM((layers, 4, rows, depth), jnp.bfloat16),
                pltpu.VMEM((nb, rows, columns), jnp.bfloat16),
                pltpu.VMEM((nb, rows, columns), jnp.bfloat16),
                pltpu.VMEM((rows, columns), jnp.float32),
                pltpu.VMEM(lower_inverse.shape[1:], jnp.float32),
                pltpu.SemaphoreType.DMA((5,)),
                pltpu.SemaphoreType.DMA((layers, nb, 3, pieces)),
                pltpu.SemaphoreType.DMA((layers, nb, pieces)),
                pltpu.SemaphoreType.DMA((layers, 2 * pieces + 1)),
                pltpu.SemaphoreType.DMA((layers, 2 * pieces + 1)),
            ],
            compiler_params=pltpu.CompilerParams(
                collective_id=0, has_side_effects=True, vmem_limit_bytes=held + 8 * 2**20
            ),
        )(factors, lower_inverse, upper_inverse, right_side)

    in_specs = (
        P(None, "blk", "grp"),
        P(None, "blk", None),
        P(None, "blk", None),
        P(None, "blk", "grp"),
    )
    return jax.shard_map(local, mesh=mesh, in_specs=in_specs, out_specs=P(None, "blk", "grp"), check_vma=False)
```
